768 devices in a mesh: vir: 64 (over x, y, core), occ: 12 (over z).
Axes of the slice: x: 4, y: 8, z: 12, core: 2. Of those that a mesh axis runs over, the one named last changes fastest.
Arguments:
- amps: bfloat16 [64, 768, 4096], P('vir'), may hold values from -6 to 6
- ints: bfloat16 [64, 36, 4096, 128], P('vir', 'occ'), may hold values from -0.015625 to 0.015625
- partners: int32 [64, 36], P('vir'), may hold values from 0 to 63, as said below
- irrep_sizes: int32 [2], replicated, may hold values from 31 to 33, as said below
- tile_slot: int32 [64], replicated, may hold values from 0 to 63, as said below
Outputs:
- residual: float32 [64, 768, 128], P('vir', 'occ')
The draws below stay inside these ranges and needn't reach their ends.
Inputs may be any that keep to these rules, and one draw needn't show every extreme that they name: `partners`: row s belongs to the tile at slot s: its first n entries, n being the size of that tile's irrep block, are the distinct tile ids of that block in some order; the remaining entries are distinct ids of the other block and name no allowed triple. A tile id is in block 0 if it is below irrep_sizes[0], else in block 1. `irrep_sizes`: one of the two sizes is 33 and the other is 31, in either order. A permutation: tile id t sits at slot tile_slot[t], the index along the first dimension of amps, ints, partners and residual.
All inputs are finite; a program needn't handle non-finite values.
Results may differ from the reference program's by a relative error of at most 0.0003.
Values sent between devices are 32-bit elements; how exact they have to be, the bound alone decides.
No kernel may reach another device: no remote copies, remote signals or barrier semaphores. Data moves between devices by JAX's collectives and lax.ppermute only.
A program may use at most 128 MiB of HBM per device.

```python
import jax
import jax.numpy as jnp
from jax import lax

CD = 4096
ROWS = 128
NOP = 768
NT = 64
BIG = 33
KP = 36


def draw_tables(key):
    key = jax.random.fold_in(key, 11)
    pick_key, perm_key, order_key = jax.random.split(key, 3)
    big_first = jax.random.randint(pick_key, (), 0, 2)
    first_size = jnp.where(big_first == 1, BIG, NT - BIG).astype(jnp.int32)
    sizes = jnp.stack([first_size, NT - first_size]).astype(jnp.int32)
    tile_slot = jax.random.permutation(perm_key, NT).astype(jnp.int32)
    slot_tile = jnp.argsort(tile_slot).astype(jnp.int32)
    tile_ids = jnp.arange(NT, dtype=jnp.int32)
    tile_irrep = (tile_ids >= first_size).astype(jnp.int32)
    own_irrep = tile_irrep[slot_tile]
    scores = jax.random.randint(order_key, (NT, NT), 0, 1 << 16) * NT + tile_ids[None, :]
    sort_keys = jnp.where(tile_irrep[None, :] == own_irrep[:, None], 0, 1 << 26) + scores
    ordering = jnp.argsort(sort_keys, axis=1).astype(jnp.int32)
    return (sizes, tile_slot, ordering[:, :KP])


def draw_partners(key, part):
    shared = draw_tables(key)
    return shared[2]


def draw_irrep_sizes(key, part):
    shared = draw_tables(key)
    return shared[0]


def draw_tile_slot(key, part):
    shared = draw_tables(key)
    return shared[1]


def block_scale(own_key, extent, pieces, low, top_value):
    level = 1.0
    for dim, shards_of in pieces:
        draws = jax.random.uniform(jax.random.fold_in(jax.random.fold_in(own_key, 6), dim), (shards_of,), jnp.float32, low / len(pieces), top_value / len(pieces))
        level = level * jnp.repeat(jnp.exp(draws), extent[dim] // shards_of).reshape((-1,) + (1,) * (len(extent) - 1 - dim))
    return level


def centred(rng, dims, width, limit, shards=(), kind=jnp.bfloat16):
    result = jax.random.normal(rng, dims, jnp.float32) * width
    if len(shards) > 0:
        result = block_scale(rng, dims, shards, -0.22, 0.18) * result
    return jnp.clip(result, min=-limit, max=limit).astype(kind)


def setup_inputs(seed: int = 0) -> dict:
    keys = jax.random.split(jax.random.key(seed), 6)
    return {
        "amps": centred(keys[0], (NT, NOP, CD), 1.0, 6.0, ((0, 64),)),
        "ints": centred(keys[1], (NT, KP, CD, ROWS), (CD * KP) ** -0.5, 0.015625, ((0, 64), (1, 12))),
        "partners": draw_partners(jax.random.fold_in(keys[5], 71), 0),
        "irrep_sizes": draw_irrep_sizes(jax.random.fold_in(keys[5], 71), 0),
        "tile_slot": draw_tile_slot(jax.random.fold_in(keys[5], 71), 0),
    }


def reference(amps, ints, partners, irrep_sizes, tile_slot):
    tile_ids = jnp.arange(NT, dtype=jnp.int32)
    slot_tile = jnp.sum(jnp.where(tile_slot[:, None] == tile_ids[None, :], tile_ids[:, None], 0), axis=0).astype(jnp.int32)
    in_second = slot_tile >= irrep_sizes[0]
    live_counts = jnp.where(in_second, irrep_sizes[1], irrep_sizes[0]).astype(jnp.int32)
    slot_order = jnp.arange(KP, dtype=jnp.int32)

    def accumulate(running, inputs):
        amp_tile, weights, partner_ids, live_count = inputs
        products = jnp.einsum('ic,kcr->kir', amp_tile.astype(jnp.float32), weights.astype(jnp.float32))
        products = jnp.where((slot_order < live_count)[:, None, None], products, jnp.float32(0.0))
        running = running.at[tile_slot[partner_ids]].add(products)
        return running, None

    running_start = jnp.zeros((NT, NOP, ROWS), jnp.float32)
    residual, _ = lax.scan(accumulate, running_start, (amps, ints, partners, live_counts))
    return residual
```

```python
import jax
import jax.numpy as jnp
from jax import lax
from jax.experimental import pallas as pl
from jax.experimental.pallas import tpu as pltpu
from jax.sharding import Mesh
from jax.sharding import PartitionSpec as P

TILES = 64
PLANES = 12
GROUP = 4
HEADS = PLANES // GROUP
PER = 3
LINES = PER * HEADS + 1
FIRST = TILES * GROUP
SECOND = TILES * HEADS
LANES = 128
CHUNK = 512
VIR = ("x", "y", "core")


def codes_row(place, sizes, slots, partners):
    slot, plane = place[0], place[1]
    own = lax.fori_loop(
        0, TILES, lambda t, own: own + jnp.where(slots[t] == slot, t, 0), jnp.int32(0)
    )
    live = jnp.where(own >= sizes[0], sizes[1], sizes[0])
    lanes = lax.broadcasted_iota(jnp.int32, (1, LANES), 1)
    row = jnp.zeros((1, LANES), jnp.float32)
    for k in range(PER):
        index = plane * PER + k
        target = jnp.where(index < live, slots[partners[index]], -1)
        row = jnp.where(lanes == target, jnp.float32(k + 1), row)
    return row


def products_kernel(place, sizes, slots, partners, amps, ints, out, total):
    step = pl.program_id(0)
    weights = jnp.concatenate([ints[k] for k in range(PER)], axis=1)
    part = jnp.dot(amps[...], weights, preferred_element_type=jnp.float32)

    @pl.when(step == 0)
    def _():
        total[...] = part

    @pl.when(step > 0)
    def _():
        total[...] += part

    @pl.when(step == pl.num_programs(0) - 1)
    def _():
        for head in range(HEADS):
            for near in range(GROUP):
                rows = pl.ds(TILES * (head * GROUP + near), TILES)
                for k in range(PER):
                    line = near * LINES + k * HEADS + head
                    out[pl.ds(line, TILES, stride=GROUP * LINES), :] = total[
                        rows, k * LANES : (k + 1) * LANES
                    ]
        row = codes_row(place, sizes, slots, partners)
        out[pl.ds(LINES - 1, FIRST, stride=LINES), :] = jnp.broadcast_to(row, (FIRST, LANES))


def products(place, sizes, slots, partners, amps, ints):
    pairs, depth = amps.shape
    scalars = pl.BlockSpec(memory_space=pltpu.SMEM)
    return pl.pallas_call(
        products_kernel,
        grid=(depth // CHUNK,),
        in_specs=[
            scalars,
            scalars,
            scalars,
            scalars,
            pl.BlockSpec((pairs, CHUNK), lambda i: (0, i)),
            pl.BlockSpec((PER, CHUNK, LANES), lambda i: (0, i, 0)),
        ],
        out_specs=pl.BlockSpec((FIRST * LINES, LANES), lambda i: (0, 0)),
        out_shape=jax.ShapeDtypeStruct((FIRST * LINES, LANES), jnp.float32),
        scratch_shapes=[pltpu.VMEM((pairs, PER * LANES), jnp.float32)],
        compiler_params=pltpu.CompilerParams(vmem_limit_bytes=56 * 1024 * 1024),
        name="products",
    )(place, sizes, slots, partners, amps, ints)


def gather_kernel(got, out):
    codes = jnp.transpose(got[pl.ds(LINES - 1, FIRST, stride=LINES), :])[:TILES]
    picks = [(codes == jnp.float32(k + 1)).astype(jnp.bfloat16) for k in range(PER)]
    for head in range(HEADS):
        sums = jnp.zeros((TILES, LANES), jnp.float32)
        for k in range(PER):
            rows = got[pl.ds(k * HEADS + head, FIRST, stride=LINES), :]
            high = rows.astype(jnp.bfloat16)
            rest = rows - high.astype(jnp.float32)
            middle = rest.astype(jnp.bfloat16)
            low = (rest - middle.astype(jnp.float32)).astype(jnp.bfloat16)
            for term in (low, middle, high):
                sums += jnp.dot(picks[k], term, preferred_element_type=jnp.float32)
        out[pl.ds(head, TILES, stride=HEADS), :] = sums


def gather(got):
    return pl.pallas_call(
        gather_kernel,
        out_shape=jax.ShapeDtypeStruct((SECOND, LANES), jnp.float32),
        compiler_params=pltpu.CompilerParams(vmem_limit_bytes=56 * 1024 * 1024),
        name="gather",
    )(got)


def finish_kernel(got, out):
    out[...] = sum(got[pl.ds(head, TILES, stride=HEADS), :] for head in range(HEADS))


def finish(got):
    return pl.pallas_call(
        finish_kernel,
        out_shape=jax.ShapeDtypeStruct((TILES, LANES), jnp.float32),
        name="finish",
    )(got)


def shards(amps, ints, partners, irrep_sizes, tile_slot):
    place = jnp.stack([lax.axis_index(VIR), lax.axis_index(("far", "near"))]).astype(jnp.int32)
    sent = products(place, irrep_sizes, tile_slot, partners[0], amps[0], ints[0])
    got = lax.all_to_all(
        sent.reshape(FIRST, LINES, 1, LANES), VIR + ("near",), 0, 0, tiled=True
    )
    sums = gather(got.reshape(FIRST * LINES, LANES))
    got = lax.all_to_all(sums.reshape(SECOND, 1, LANES), VIR + ("far",), 0, 0, tiled=True)
    return finish(got.reshape(SECOND, LANES))[None]


def solution(mesh):
    fine = Mesh(
        mesh.devices.reshape(4, 8, 2, HEADS, GROUP), ("x", "y", "core", "far", "near")
    )
    occ = ("far", "near")
    in_specs = (P(VIR, None, None), P(VIR, occ, None, None), P(VIR, None), P(), P())
    out_specs = P(VIR, occ, None)
    return jax.shard_map(shards, mesh=fine, in_specs=in_specs, out_specs=out_specs, check_vma=False)
```

```python
import jax
import jax.numpy as jnp
from jax import lax
from jax.experimental import pallas as pl
from jax.experimental.pallas import tpu as pltpu
from jax.sharding import Mesh
from jax.sharding import PartitionSpec as P

TILES = 64
PLANES = 12
NEAR_Y = 2
NEAR_Z = 3
FAR_Y = 8 // NEAR_Y
FAR_Z = PLANES // NEAR_Z
PER = 3
PIECES = 8 * NEAR_Y
EACH = TILES // PIECES
FIRST = PIECES * NEAR_Z
THIRD = PIECES * FAR_Z
PARTS = FAR_Y * FAR_Z
LINES = PER * FAR_Z * EACH + 1
LANES = 128
CHUNK = 512
HALF = 384
ROOM = 56 * 1024 * 1024
SMALL = 16 * 1024 * 1024
VIR = ("x", "far_y", "near_y", "core")
OCC = ("far_z", "near_z")


def codes_row(sizes, slots, partners):
    y = lax.axis_index("far_y") * NEAR_Y + lax.axis_index("near_y")
    slot = (lax.axis_index("x") * 8 + y) * 2 + lax.axis_index("core")
    plane = lax.axis_index("far_z") * NEAR_Z + lax.axis_index("near_z")
    own = lax.fori_loop(
        0, TILES, lambda t, own: own + jnp.where(slots[t] == slot, t, 0), jnp.int32(0)
    )
    live = jnp.where(own >= sizes[0], sizes[1], sizes[0])
    lanes = lax.broadcasted_iota(jnp.int32, (1, LANES), 1)
    far, piece = lanes // PIECES, lanes % PIECES
    x, low = piece // (2 * NEAR_Y), piece % (2 * NEAR_Y)
    slot_of = (x * FAR_Y + far) * 2 * NEAR_Y + low
    slot_of = jnp.where(lanes < TILES, slot_of, -2)
    row = jnp.zeros((1, LANES), jnp.float32)
    for k in range(PER):
        index = plane * PER + k
        target = jnp.where(index < live, slots[partners[index]], -1)
        row = jnp.where(slot_of == target, jnp.float32(k + 1), row)
    return row


def products_kernel(sizes, slots, partners, amps, ints, out, left, right, total, sems):
    depth = amps.shape[1]
    copies = []
    for step in range(depth // CHUNK):
        part = pl.ds(step * CHUNK, CHUNK)
        copies.append(
            (
                pltpu.make_async_copy(amps.at[:, part], left.at[:, part], sems.at[0, step]),
                pltpu.make_async_copy(ints.at[:, part], right.at[:, part], sems.at[1, step]),
            )
        )
    for pair in copies:
        for copy in pair:
            copy.start()
    row = codes_row(sizes, slots, partners)
    out[pl.ds(LINES - 1, FIRST, stride=LINES), :] = jnp.broadcast_to(row, (FIRST, LANES))
    for step, pair in enumerate(copies):
        for copy in pair:
            copy.wait()
        part = pl.ds(step * CHUNK, CHUNK)
        weights = jnp.concatenate([right[k, part, :] for k in range(PER)], axis=1)
        for half in range(2):
            rows = pl.ds(half * HALF, HALF)
            now = jnp.dot(left[rows, part], weights, preferred_element_type=jnp.float32)
            for k in range(PER):
                term = now[:, k * LANES : (k + 1) * LANES]
                total[k, rows, :] = term if step == 0 else total[k, rows, :] + term
    for far in range(FAR_Z):
        for near in range(NEAR_Z):
            for k in range(PER):
                for j in range(EACH):
                    start = TILES * (far * NEAR_Z + near) + j
                    line = near * LINES + (k * FAR_Z + far) * EACH + j
                    out[pl.ds(line, PIECES, stride=NEAR_Z * LINES), :] = total[
                        k, pl.ds(start, PIECES, stride=EACH), :
                    ]


def products(sizes, slots, partners, amps, ints):
    pairs, depth = amps.shape
    scalars = pl.BlockSpec(memory_space=pltpu.SMEM)
    return pl.pallas_call(
        products_kernel,
        in_specs=[scalars] * 3 + [pl.BlockSpec(memory_space=pl.ANY)] * 2,
        out_specs=pl.BlockSpec(memory_space=pltpu.VMEM),
        out_shape=jax.ShapeDtypeStruct((FIRST * LINES, LANES), jnp.float32),
        scratch_shapes=[
            pltpu.VMEM((pairs, depth), jnp.bfloat16),
            pltpu.VMEM((PER, depth, LANES), jnp.bfloat16),
            pltpu.VMEM((PER, pairs, LANES), jnp.float32),
            pltpu.SemaphoreType.DMA((2, depth // CHUNK)),
        ],
        compiler_params=pltpu.CompilerParams(vmem_limit_bytes=ROOM),
        name="products",
    )(sizes, slots, partners, amps, ints)


def gather_kernel(got, out):
    codes = jnp.transpose(got[pl.ds(LINES - 1, FIRST, stride=LINES), :])[:TILES]
    picks = [(codes == jnp.float32(k + 1)).astype(jnp.float32) for k in range(PER)]
    picks = jnp.concatenate(picks * 3, axis=1).astype(jnp.bfloat16)
    for far in range(FAR_Z):
        for j in range(EACH):
            rows = [
                got[pl.ds((k * FAR_Z + far) * EACH + j, FIRST, stride=LINES), :]
                for k in range(PER)
            ]
            rows = jnp.concatenate(rows, axis=0)
            high = rows.astype(jnp.bfloat16)
            rest = rows - high.astype(jnp.float32)
            middle = rest.astype(jnp.bfloat16)
            low = (rest - middle.astype(jnp.float32)).astype(jnp.bfloat16)
            terms = jnp.concatenate([low, middle, high], axis=0)
            sums = jnp.dot(picks, terms, preferred_element_type=jnp.float32)
            for far_y in range(FAR_Y):
                start = (far_y * FAR_Z + far) * TILES + j
                out[pl.ds(start, PIECES, stride=EACH), :] = sums[
                    far_y * PIECES : (far_y + 1) * PIECES
                ]


def gather(got):
    return pl.pallas_call(
        gather_kernel,
        out_shape=jax.ShapeDtypeStruct((PARTS * TILES, LANES), jnp.float32),
        compiler_params=pltpu.CompilerParams(vmem_limit_bytes=SMALL),
        name="gather",
    )(got)


def add_kernel(got, out):
    rows = out.shape[0]
    out[...] = sum(got[pl.ds(start, rows), :] for start in range(0, got.shape[0], rows))


def add(got, parts):
    return pl.pallas_call(
        add_kernel,
        out_shape=jax.ShapeDtypeStruct((got.shape[0] // parts, LANES), jnp.float32),
        compiler_params=pltpu.CompilerParams(vmem_limit_bytes=SMALL),
        name="add",
    )(got)


def exchange(rows, axes, devices):
    each = rows.shape[0] // devices
    sent = rows.reshape(devices, each, 1, LANES)
    return lax.all_to_all(sent, axes, 0, 0, tiled=True).reshape(rows.shape)


def shards(amps, ints, partners, irrep_sizes, tile_slot):
    sent = products(irrep_sizes, tile_slot, partners[0], amps[0], ints[0])
    got = exchange(sent, ("x", "near_y", "core", "near_z"), FIRST)
    sums = gather(got)
    sums = add(exchange(sums, ("far_y",), FAR_Y), FAR_Y)
    got = exchange(sums, ("far_z", "x", "near_y", "core"), THIRD)
    return add(got, FAR_Z)[None]


def solution(mesh):
    fine = Mesh(mesh.devices.reshape(4, FAR_Y, NEAR_Y, 2, FAR_Z, NEAR_Z), VIR + OCC)
    in_specs = (P(VIR, None, None), P(VIR, OCC, None, None), P(VIR, None), P(), P())
    out_specs = P(VIR, OCC, None)
    return jax.shard_map(shards, mesh=fine, in_specs=in_specs, out_specs=out_specs, check_vma=False)
```

```python
import jax
import jax.numpy as jnp
from jax import lax
from jax.experimental import pallas as pl
from jax.experimental.pallas import tpu as pltpu
from jax.sharding import Mesh
from jax.sharding import PartitionSpec as P

TILES = 64
PLANES = 12
NEAR_Y = 2
NEAR_Z = 3
FAR_Y = 8 // NEAR_Y
FAR_Z = PLANES // NEAR_Z
PER = 3
PIECES = 8 * NEAR_Y
EACH = TILES // PIECES
FIRST = PIECES * NEAR_Z
PARTS = FAR_Y * FAR_Z
LINES = PER * FAR_Z * EACH + 1
LANES = 128
CHUNK = 512
HALF = 384
ROOM = 56 * 1024 * 1024
SMALL = 16 * 1024 * 1024
VIR = ("x", "far_y", "near_y", "core")
OCC = ("far_z", "near_z")


def codes_row(sizes, slots, partners):
    y = lax.axis_index("far_y") * NEAR_Y + lax.axis_index("near_y")
    slot = (lax.axis_index("x") * 8 + y) * 2 + lax.axis_index("core")
    plane = lax.axis_index("far_z") * NEAR_Z + lax.axis_index("near_z")
    own = lax.fori_loop(
        0, TILES, lambda t, own: own + jnp.where(slots[t] == slot, t, 0), jnp.int32(0)
    )
    live = jnp.where(own >= sizes[0], sizes[1], sizes[0])
    lanes = lax.broadcasted_iota(jnp.int32, (1, LANES), 1)
    far, piece = lanes // PIECES, lanes % PIECES
    x, low = piece // (2 * NEAR_Y), piece % (2 * NEAR_Y)
    slot_of = (x * FAR_Y + far) * 2 * NEAR_Y + low
    slot_of = jnp.where(lanes < TILES, slot_of, -2)
    row = jnp.zeros((1, LANES), jnp.float32)
    for k in range(PER):
        index = plane * PER + k
        target = jnp.where(index < live, slots[partners[index]], -1)
        row = jnp.where(slot_of == target, jnp.float32(k + 1), row)
    return row


def products_kernel(sizes, slots, partners, amps, ints, out, left, right, total, sems):
    depth = amps.shape[1]
    copies = []
    for step in range(depth // CHUNK):
        part = pl.ds(step * CHUNK, CHUNK)
        copies.append(
            (
                pltpu.make_async_copy(amps.at[:, part], left.at[:, part], sems.at[0, step]),
                pltpu.make_async_copy(ints.at[:, part], right.at[:, part], sems.at[1, step]),
            )
        )
    for pair in copies:
        for copy in pair:
            copy.start()
    row = codes_row(sizes, slots, partners)
    out[pl.ds(LINES - 1, FIRST, stride=LINES), :] = jnp.broadcast_to(row, (FIRST, LANES))
    for step, pair in enumerate(copies):
        for copy in pair:
            copy.wait()
        part = pl.ds(step * CHUNK, CHUNK)
        weights = jnp.concatenate([right[k, part, :] for k in range(PER)], axis=1)
        for half in range(2):
            rows = pl.ds(half * HALF, HALF)
            now = jnp.dot(left[rows, part], weights, preferred_element_type=jnp.float32)
            for k in range(PER):
                term = now[:, k * LANES : (k + 1) * LANES]
                total[k, rows, :] = term if step == 0 else total[k, rows, :] + term
    for far in range(FAR_Z):
        for near in range(NEAR_Z):
            for k in range(PER):
                for j in range(EACH):
                    start = TILES * (far * NEAR_Z + near) + j
                    line = near * LINES + (k * FAR_Z + far) * EACH + j
                    out[pl.ds(line, PIECES, stride=NEAR_Z * LINES), :] = total[
                        k, pl.ds(start, PIECES, stride=EACH), :
                    ]


def products(sizes, slots, partners, amps, ints):
    pairs, depth = amps.shape
    scalars = pl.BlockSpec(memory_space=pltpu.SMEM)
    return pl.pallas_call(
        products_kernel,
        in_specs=[scalars] * 3 + [pl.BlockSpec(memory_space=pl.ANY)] * 2,
        out_specs=pl.BlockSpec(memory_space=pltpu.VMEM),
        out_shape=jax.ShapeDtypeStruct((FIRST * LINES, LANES), jnp.float32),
        scratch_shapes=[
            pltpu.VMEM((pairs, depth), jnp.bfloat16),
            pltpu.VMEM((PER, depth, LANES), jnp.bfloat16),
            pltpu.VMEM((PER, pairs, LANES), jnp.float32),
            pltpu.SemaphoreType.DMA((2, depth // CHUNK)),
        ],
        compiler_params=pltpu.CompilerParams(vmem_limit_bytes=ROOM),
        name="products",
    )(sizes, slots, partners, amps, ints)


def gather_kernel(got, out):
    codes = jnp.transpose(got[pl.ds(LINES - 1, FIRST, stride=LINES), :])[:TILES]
    picks = [(codes == jnp.float32(k + 1)).astype(jnp.float32) for k in range(PER)]
    picks = jnp.concatenate(picks * 3, axis=1).astype(jnp.bfloat16)
    for far in range(FAR_Z):
        for j in range(EACH):
            rows = [
                got[pl.ds((k * FAR_Z + far) * EACH + j, FIRST, stride=LINES), :]
                for k in range(PER)
            ]
            rows = jnp.concatenate(rows, axis=0)
            high = rows.astype(jnp.bfloat16)
            rest = rows - high.astype(jnp.float32)
            middle = rest.astype(jnp.bfloat16)
            low = (rest - middle.astype(jnp.float32)).astype(jnp.bfloat16)
            terms = jnp.concatenate([low, middle, high], axis=0)
            sums = jnp.dot(picks, terms, preferred_element_type=jnp.float32)
            for far_y in range(FAR_Y):
                start = (far_y * FAR_Z + far) * TILES + j
                out[pl.ds(start, PIECES, stride=EACH), :] = sums[
                    far_y * PIECES : (far_y + 1) * PIECES
                ]


def gather(got):
    return pl.pallas_call(
        gather_kernel,
        out_shape=jax.ShapeDtypeStruct((PARTS * TILES, LANES), jnp.float32),
        compiler_params=pltpu.CompilerParams(vmem_limit_bytes=SMALL),
        name="gather",
    )(got)


def add_kernel(got, out):
    out[...] = sum(got[pl.ds(part * TILES, TILES), :] for part in range(PARTS))


def add(got):
    return pl.pallas_call(
        add_kernel,
        out_shape=jax.ShapeDtypeStruct((TILES, LANES), jnp.float32),
        compiler_params=pltpu.CompilerParams(vmem_limit_bytes=SMALL),
        name="add",
    )(got)


def exchange(rows, axes, devices):
    each = rows.shape[0] // devices
    sent = rows.reshape(devices, each, 1, LANES)
    return lax.all_to_all(sent, axes, 0, 0, tiled=True).reshape(rows.shape)


def shards(amps, ints, partners, irrep_sizes, tile_slot):
    sent = products(irrep_sizes, tile_slot, partners[0], amps[0], ints[0])
    got = exchange(sent, ("x", "near_y", "core", "near_z"), FIRST)
    sums = gather(got)
    sums = add(exchange(sums, ("far_y", "far_z"), PARTS))
    return exchange(sums, ("x", "near_y", "core"), PIECES)[None]


def solution(mesh):
    fine = Mesh(mesh.devices.reshape(4, FAR_Y, NEAR_Y, 2, FAR_Z, NEAR_Z), VIR + OCC)
    in_specs = (P(VIR, None, None), P(VIR, OCC, None, None), P(VIR, None), P(), P())
    out_specs = P(VIR, OCC, None)
    return jax.shard_map(shards, mesh=fine, in_specs=in_specs, out_specs=out_specs, check_vma=False)
```

```python
import jax
import jax.numpy as jnp
from jax import lax
from jax.experimental import pallas as pl
from jax.experimental.pallas import tpu as pltpu
from jax.sharding import Mesh
from jax.sharding import PartitionSpec as P

TILES = 64
PLANES = 12
NEAR_Y = 2
NEAR_Z = 3
FAR_Y = 8 // NEAR_Y
FAR_Z = PLANES // NEAR_Z
PER = 3
PIECES = 8 * NEAR_Y
EACH = TILES // PIECES
FIRST = PIECES * NEAR_Z
LINES = PER * FAR_Z * EACH + 1
LANES = 128
CHUNK = 512
HALF = 384
ROOM = 56 * 1024 * 1024
SMALL = 16 * 1024 * 1024
VIR = ("x", "far_y", "near_y", "core")
OCC = ("far_z", "near_z")


def codes_row(sizes, slots, partners):
    y = lax.axis_index("far_y") * NEAR_Y + lax.axis_index("near_y")
    slot = (lax.axis_index("x") * 8 + y) * 2 + lax.axis_index("core")
    plane = lax.axis_index("far_z") * NEAR_Z + lax.axis_index("near_z")
    own = lax.fori_loop(
        0, TILES, lambda t, own: own + jnp.where(slots[t] == slot, t, 0), jnp.int32(0)
    )
    live = jnp.where(own >= sizes[0], sizes[1], sizes[0])
    lanes = lax.broadcasted_iota(jnp.int32, (1, LANES), 1)
    far, piece = lanes // PIECES, lanes % PIECES
    x, low = piece // (2 * NEAR_Y), piece % (2 * NEAR_Y)
    slot_of = (x * FAR_Y + far) * 2 * NEAR_Y + low
    slot_of = jnp.where(lanes < TILES, slot_of, -2)
    row = jnp.zeros((1, LANES), jnp.float32)
    for k in range(PER):
        index = plane * PER + k
        target = jnp.where(index < live, slots[partners[index]], -1)
        row = jnp.where(slot_of == target, jnp.float32(k + 1), row)
    return row


def products_kernel(sizes, slots, partners, amps, ints, out, left, right, total, sems):
    depth = amps.shape[1]
    copies = []
    for step in range(depth // CHUNK):
        part = pl.ds(step * CHUNK, CHUNK)
        copies.append(
            (
                pltpu.make_async_copy(amps.at[:, part], left.at[:, part], sems.at[0, step]),
                pltpu.make_async_copy(ints.at[:, part], right.at[:, part], sems.at[1, step]),
            )
        )
    for pair in copies:
        for copy in pair:
            copy.start()
    row = codes_row(sizes, slots, partners)
    out[pl.ds(LINES - 1, FIRST, stride=LINES), :] = jnp.broadcast_to(row, (FIRST, LANES))
    for step, pair in enumerate(copies):
        for copy in pair:
            copy.wait()
        part = pl.ds(step * CHUNK, CHUNK)
        weights = jnp.concatenate([right[k, part, :] for k in range(PER)], axis=1)
        for half in range(2):
            rows = pl.ds(half * HALF, HALF)
            now = jnp.dot(left[rows, part], weights, preferred_element_type=jnp.float32)
            for k in range(PER):
                term = now[:, k * LANES : (k + 1) * LANES]
                total[k, rows, :] = term if step == 0 else total[k, rows, :] + term
    for far in range(FAR_Z):
        for near in range(NEAR_Z):
            for k in range(PER):
                for j in range(EACH):
                    start = TILES * (far * NEAR_Z + near) + j
                    line = near * LINES + (k * FAR_Z + far) * EACH + j
                    out[pl.ds(line, PIECES, stride=NEAR_Z * LINES), :] = total[
                        k, pl.ds(start, PIECES, stride=EACH), :
                    ]


def products(sizes, slots, partners, amps, ints):
    pairs, depth = amps.shape
    scalars = pl.BlockSpec(memory_space=pltpu.SMEM)
    return pl.pallas_call(
        products_kernel,
        in_specs=[scalars] * 3 + [pl.BlockSpec(memory_space=pl.ANY)] * 2,
        out_specs=pl.BlockSpec(memory_space=pltpu.VMEM),
        out_shape=jax.ShapeDtypeStruct((FIRST * LINES, LANES), jnp.float32),
        scratch_shapes=[
            pltpu.VMEM((pairs, depth), jnp.bfloat16),
            pltpu.VMEM((PER, depth, LANES), jnp.bfloat16),
            pltpu.VMEM((PER, pairs, LANES), jnp.float32),
            pltpu.SemaphoreType.DMA((2, depth // CHUNK)),
        ],
        compiler_params=pltpu.CompilerParams(vmem_limit_bytes=ROOM),
        name="products",
    )(sizes, slots, partners, amps, ints)


def gather_kernel(got, out):
    codes = jnp.transpose(got[pl.ds(LINES - 1, FIRST, stride=LINES), :])[:TILES]
    picks = [(codes == jnp.float32(k + 1)).astype(jnp.float32) for k in range(PER)]
    picks = jnp.concatenate(picks * 3, axis=1).astype(jnp.bfloat16)
    for far in range(FAR_Z):
        for j in range(EACH):
            rows = [
                got[pl.ds((k * FAR_Z + far) * EACH + j, FIRST, stride=LINES), :]
                for k in range(PER)
            ]
            rows = jnp.concatenate(rows, axis=0)
            high = rows.astype(jnp.bfloat16)
            rest = rows - high.astype(jnp.float32)
            middle = rest.astype(jnp.bfloat16)
            low = (rest - middle.astype(jnp.float32)).astype(jnp.bfloat16)
            terms = jnp.concatenate([low, middle, high], axis=0)
            sums = jnp.dot(picks, terms, preferred_element_type=jnp.float32)
            out[pl.ds(far * EACH + j, TILES, stride=FAR_Z * EACH), :] = sums


def gather(got):
    return pl.pallas_call(
        gather_kernel,
        out_shape=jax.ShapeDtypeStruct((TILES * FAR_Z * EACH, LANES), jnp.float32),
        compiler_params=pltpu.CompilerParams(vmem_limit_bytes=SMALL),
        name="gather",
    )(got)


def add_kernel(got, out):
    for far in range(FAR_Z):
        for j in range(EACH):
            line = far * EACH + j
            rows = [
                got[pl.ds(y * PIECES * FAR_Z * EACH + line, PIECES, stride=FAR_Z * EACH), :]
                for y in range(FAR_Y)
            ]
            out[pl.ds(far * TILES + j, PIECES, stride=EACH), :] = sum(rows[1:], rows[0])


def finish_kernel(got, out):
    parts = [got[pl.ds(far * TILES, TILES), :] for far in range(FAR_Z)]
    out[...] = sum(parts[1:], parts[0])


def add(kernel, got, rows):
    return pl.pallas_call(
        kernel,
        out_shape=jax.ShapeDtypeStruct((rows, LANES), jnp.float32),
        compiler_params=pltpu.CompilerParams(vmem_limit_bytes=SMALL),
        name="add",
    )(got)


def exchange(rows, axes, devices):
    each = rows.shape[0] // devices
    sent = rows.reshape(devices, each, 1, LANES)
    return lax.all_to_all(sent, axes, 0, 0, tiled=True).reshape(rows.shape)


def shards(amps, ints, partners, irrep_sizes, tile_slot):
    sent = products(irrep_sizes, tile_slot, partners[0], amps[0], ints[0])
    got = exchange(sent, ("x", "near_y", "core", "near_z"), FIRST)
    sums = gather(got)
    got = exchange(sums, ("far_y", "x", "near_y", "core"), TILES)
    sums = add(add_kernel, got, FAR_Z * TILES)
    got = exchange(sums, ("far_z",), FAR_Z)
    return add(finish_kernel, got, TILES)[None]


def solution(mesh):
    fine = Mesh(mesh.devices.reshape(4, FAR_Y, NEAR_Y, 2, FAR_Z, NEAR_Z), VIR + OCC)
    in_specs = (P(VIR, None, None), P(VIR, OCC, None, None), P(VIR, None), P(), P())
    out_specs = P(VIR, OCC, None)
    return jax.shard_map(shards, mesh=fine, in_specs=in_specs, out_specs=out_specs, check_vma=False)
```

```python
import jax
import jax.numpy as jnp
from jax import lax
from jax.experimental import pallas as pl
from jax.experimental.pallas import tpu as pltpu
from jax.sharding import Mesh
from jax.sharding import PartitionSpec as P

TILES = 64
PLANES = 12
NEAR_Y = 2
NEAR_Z = 3
FAR_Y = 8 // NEAR_Y
FAR_Z = PLANES // NEAR_Z
PER = 3
PIECES = 8 * NEAR_Y
EACH = TILES // PIECES
FIRST = PIECES * NEAR_Z
LINES = PER * FAR_Z * EACH + 1
LANES = 128
DEPTHS = (512, 1024, 1024, 1024, 256, 256)
STARTS = tuple(sum(DEPTHS[:step]) for step in range(len(DEPTHS)))
HALF = 384
ROOM = 56 * 1024 * 1024
SMALL = 16 * 1024 * 1024
VIR = ("x", "far_y", "near_y", "core")
OCC = ("far_z", "near_z")


def codes_row(sizes, slots, partners):
    y = lax.axis_index("far_y") * NEAR_Y + lax.axis_index("near_y")
    slot = (lax.axis_index("x") * 8 + y) * 2 + lax.axis_index("core")
    plane = lax.axis_index("far_z") * NEAR_Z + lax.axis_index("near_z")
    own = lax.fori_loop(
        0, TILES, lambda t, own: own + jnp.where(slots[t] == slot, t, 0), jnp.int32(0)
    )
    live = jnp.where(own >= sizes[0], sizes[1], sizes[0])
    lanes = lax.broadcasted_iota(jnp.int32, (1, LANES), 1)
    far, piece = lanes // PIECES, lanes % PIECES
    x, core = piece // 2 % 4, piece % 2
    slot_of = (x * 8 + far * NEAR_Y + piece // 8) * 2 + core
    slot_of = jnp.where(lanes < TILES, slot_of, -2)
    row = jnp.zeros((1, LANES), jnp.float32)
    for k in range(PER):
        index = plane * PER + k
        target = jnp.where(index < live, slots[partners[index]], -1)
        row = jnp.where(slot_of == target, jnp.float32(k + 1), row)
    return row


def products_kernel(tables, amps, ints, out, left, right, total, held, sems, table_sems):
    copies = []
    for step, (start, depth) in enumerate(zip(STARTS, DEPTHS)):
        part = pl.ds(start, depth)
        copies.append(
            (
                pltpu.make_async_copy(amps.at[:, part], left.at[:, part], sems.at[0, step]),
                pltpu.make_async_copy(ints.at[:, part], right.at[:, part], sems.at[1, step]),
            )
        )
    small = [
        pltpu.make_async_copy(tables[i], held[i], table_sems.at[i]) for i in range(len(tables))
    ]
    for copy in copies[0]:
        copy.start()
    for copy in small:
        copy.start()
    for pair in copies[1:]:
        for copy in pair:
            copy.start()
    for copy in small:
        copy.wait()
    row = codes_row(*held)
    out[pl.ds(LINES - 1, FIRST, stride=LINES), :] = jnp.broadcast_to(row, (FIRST, LANES))
    for step, pair in enumerate(copies):
        for copy in pair:
            copy.wait()
        part = pl.ds(STARTS[step], DEPTHS[step])
        weights = jnp.concatenate([right[k, part, :] for k in range(PER)], axis=1)
        for half in range(2):
            rows = pl.ds(half * HALF, HALF)
            now = jnp.dot(left[rows, part], weights, preferred_element_type=jnp.float32)
            for k in range(PER):
                term = now[:, k * LANES : (k + 1) * LANES]
                total[k, rows, :] = term if step == 0 else total[k, rows, :] + term
    for far in range(FAR_Z):
        for near in range(NEAR_Z):
            for k in range(PER):
                for j in range(EACH):
                    start = TILES * (far * NEAR_Z + near) + j
                    line = near * PIECES * LINES + (k * FAR_Z + far) * EACH + j
                    out[pl.ds(line, PIECES, stride=LINES), :] = total[
                        k, pl.ds(start, PIECES, stride=EACH), :
                    ]


def products(sizes, slots, partners, amps, ints):
    pairs, depth = amps.shape
    anywhere = pl.BlockSpec(memory_space=pl.ANY)
    tables = (sizes, slots, partners)
    return pl.pallas_call(
        products_kernel,
        in_specs=[(anywhere,) * 3, anywhere, anywhere],
        out_specs=pl.BlockSpec(memory_space=pltpu.VMEM),
        out_shape=jax.ShapeDtypeStruct((FIRST * LINES, LANES), jnp.float32),
        scratch_shapes=[
            pltpu.VMEM((pairs, depth), jnp.bfloat16),
            pltpu.VMEM((PER, depth, LANES), jnp.bfloat16),
            pltpu.VMEM((PER, pairs, LANES), jnp.float32),
            [pltpu.SMEM(table.shape, jnp.int32) for table in tables],
            pltpu.SemaphoreType.DMA((2, len(DEPTHS))),
            pltpu.SemaphoreType.DMA((len(tables),)),
        ],
        compiler_params=pltpu.CompilerParams(vmem_limit_bytes=ROOM),
        name="products",
    )(tables, amps, ints)


def gather_kernel(got, out):
    codes = jnp.transpose(got[pl.ds(LINES - 1, FIRST, stride=LINES), :])[:TILES]
    picks = [(codes == jnp.float32(k + 1)).astype(jnp.float32) for k in range(PER)]
    picks = jnp.concatenate(picks * 3, axis=1).astype(jnp.bfloat16)
    for far in range(FAR_Z):
        for j in range(EACH):
            rows = [
                got[pl.ds((k * FAR_Z + far) * EACH + j, FIRST, stride=LINES), :]
                for k in range(PER)
            ]
            rows = jnp.concatenate(rows, axis=0)
            high = rows.astype(jnp.bfloat16)
            rest = rows - high.astype(jnp.float32)
            middle = rest.astype(jnp.bfloat16)
            low = (rest - middle.astype(jnp.float32)).astype(jnp.bfloat16)
            terms = jnp.concatenate([low, middle, high], axis=0)
            sums = jnp.dot(picks, terms, preferred_element_type=jnp.float32)
            out[pl.ds(far * EACH + j, TILES, stride=FAR_Z * EACH), :] = sums


def gather(got):
    return pl.pallas_call(
        gather_kernel,
        out_shape=jax.ShapeDtypeStruct((TILES * FAR_Z * EACH, LANES), jnp.float32),
        compiler_params=pltpu.CompilerParams(vmem_limit_bytes=SMALL),
        name="gather",
    )(got)


def add_kernel(got, out):
    for far in range(FAR_Z):
        for j in range(EACH):
            line = far * EACH + j
            rows = [
                got[pl.ds(y * PIECES * FAR_Z * EACH + line, PIECES, stride=FAR_Z * EACH), :]
                for y in range(FAR_Y)
            ]
            out[pl.ds(far * TILES + j, PIECES, stride=EACH), :] = sum(rows[1:], rows[0])


def finish_kernel(got, out):
    parts = [got[pl.ds(far * TILES, TILES), :] for far in range(FAR_Z)]
    out[...] = sum(parts[1:], parts[0])


def add(kernel, got, rows):
    return pl.pallas_call(
        kernel,
        out_shape=jax.ShapeDtypeStruct((rows, LANES), jnp.float32),
        compiler_params=pltpu.CompilerParams(vmem_limit_bytes=SMALL),
        name="add",
    )(got)


def exchange(rows, axes, devices):
    each = rows.shape[0] // devices
    sent = rows.reshape(devices, each, 1, LANES)
    return lax.all_to_all(sent, axes, 0, 0, tiled=True).reshape(rows.shape)


def shards(amps, ints, partners, irrep_sizes, tile_slot):
    sent = products(irrep_sizes, tile_slot, partners[0], amps[0], ints[0])
    got = exchange(sent, ("near_z", "near_y", "x", "core"), FIRST)
    sums = gather(got)
    got = exchange(sums, ("far_y", "near_y", "x", "core"), TILES)
    sums = add(add_kernel, got, FAR_Z * TILES)
    got = exchange(sums, ("far_z",), FAR_Z)
    return add(finish_kernel, got, TILES)[None]


def solution(mesh):
    fine = Mesh(mesh.devices.reshape(4, FAR_Y, NEAR_Y, 2, FAR_Z, NEAR_Z), VIR + OCC)
    in_specs = (P(VIR, None, None), P(VIR, OCC, None, None), P(VIR, None), P(), P())
    out_specs = P(VIR, OCC, None)
    return jax.shard_map(shards, mesh=fine, in_specs=in_specs, out_specs=out_specs, check_vma=False)
```

```python
import jax
import jax.numpy as jnp
from jax import lax
from jax.experimental import pallas as pl
from jax.experimental.pallas import tpu as pltpu
from jax.sharding import Mesh
from jax.sharding import PartitionSpec as P

TILES = 64
PLANES = 12
NEAR_Y = 2
NEAR_Z = 3
FAR_Y = 8 // NEAR_Y
FAR_Z = PLANES // NEAR_Z
PER = 3
PIECES = 8 * NEAR_Y
EACH = TILES // PIECES
FIRST = PIECES * NEAR_Z
LINES = PER * FAR_Z * EACH + 1
LANES = 128
DEPTHS = (512, 1024, 1024, 1024, 256, 256)
STARTS = tuple(sum(DEPTHS[:step]) for step in range(len(DEPTHS)))
HALF = 384
ROOM = 56 * 1024 * 1024
SMALL = 16 * 1024 * 1024
VIR = ("x", "far_y", "near_y", "core")
OCC = ("far_z", "near_z")


def codes_row(sizes, slots, partners):
    y = lax.axis_index("far_y") * NEAR_Y + lax.axis_index("near_y")
    slot = (lax.axis_index("x") * 8 + y) * 2 + lax.axis_index("core")
    plane = lax.axis_index("far_z") * NEAR_Z + lax.axis_index("near_z")
    own = lax.fori_loop(
        0, TILES, lambda t, own: own + jnp.where(slots[t] == slot, t, 0), jnp.int32(0)
    )
    live = jnp.where(own >= sizes[0], sizes[1], sizes[0])
    lanes = lax.broadcasted_iota(jnp.int32, (1, LANES), 1)
    slot_of = (lanes // 2 % 4 * 8 + lanes // 8) * 2 + lanes % 2
    slot_of = jnp.where(lanes < TILES, slot_of, -2)
    row = jnp.zeros((1, LANES), jnp.float32)
    for k in range(PER):
        index = plane * PER + k
        target = jnp.where(index < live, slots[partners[index]], -1)
        row = jnp.where(slot_of == target, jnp.float32(k + 1), row)
    return row


def products_kernel(tables, amps, ints, out, left, right, total, held, sems, table_sems):
    copies = []
    for step, (start, depth) in enumerate(zip(STARTS, DEPTHS)):
        part = pl.ds(start, depth)
        copies.append(
            (
                pltpu.make_async_copy(amps.at[:, part], left.at[:, part], sems.at[0, step]),
                pltpu.make_async_copy(ints.at[:, part], right.at[:, part], sems.at[1, step]),
            )
        )
    small = [
        pltpu.make_async_copy(tables[i], held[i], table_sems.at[i]) for i in range(len(tables))
    ]
    for copy in copies[0]:
        copy.start()
    for copy in small:
        copy.start()
    for pair in copies[1:]:
        for copy in pair:
            copy.start()
    for copy in small:
        copy.wait()
    row = codes_row(*held)
    out[pl.ds(LINES - 1, FIRST, stride=LINES), :] = jnp.broadcast_to(row, (FIRST, LANES))
    for step, pair in enumerate(copies):
        for copy in pair:
            copy.wait()
        part = pl.ds(STARTS[step], DEPTHS[step])
        weights = jnp.concatenate([right[k, part, :] for k in range(PER)], axis=1)
        for half in range(2):
            rows = pl.ds(half * HALF, HALF)
            now = jnp.dot(left[rows, part], weights, preferred_element_type=jnp.float32)
            for k in range(PER):
                term = now[:, k * LANES : (k + 1) * LANES]
                total[k, rows, :] = term if step == 0 else total[k, rows, :] + term
    for far in range(FAR_Z):
        for near in range(NEAR_Z):
            for k in range(PER):
                for j in range(EACH):
                    start = TILES * (far * NEAR_Z + near) + j
                    line = near * PIECES * LINES + (k * FAR_Z + far) * EACH + j
                    out[pl.ds(line, PIECES, stride=LINES), :] = total[
                        k, pl.ds(start, PIECES, stride=EACH), :
                    ]


def products(sizes, slots, partners, amps, ints):
    pairs, depth = amps.shape
    anywhere = pl.BlockSpec(memory_space=pl.ANY)
    tables = (sizes, slots, partners)
    return pl.pallas_call(
        products_kernel,
        in_specs=[(anywhere,) * 3, anywhere, anywhere],
        out_specs=pl.BlockSpec(memory_space=pltpu.VMEM),
        out_shape=jax.ShapeDtypeStruct((FIRST * LINES, LANES), jnp.float32),
        scratch_shapes=[
            pltpu.VMEM((pairs, depth), jnp.bfloat16),
            pltpu.VMEM((PER, depth, LANES), jnp.bfloat16),
            pltpu.VMEM((PER, pairs, LANES), jnp.float32),
            [pltpu.SMEM(table.shape, jnp.int32) for table in tables],
            pltpu.SemaphoreType.DMA((2, len(DEPTHS))),
            pltpu.SemaphoreType.DMA((len(tables),)),
        ],
        compiler_params=pltpu.CompilerParams(vmem_limit_bytes=ROOM),
        name="products",
    )(tables, amps, ints)


def gather_kernel(got, out):
    codes = jnp.transpose(got[pl.ds(LINES - 1, FIRST, stride=LINES), :])[:TILES]
    picks = [(codes == jnp.float32(k + 1)).astype(jnp.float32) for k in range(PER)]
    picks = jnp.concatenate(picks * 3, axis=1).astype(jnp.bfloat16)
    for far in range(FAR_Z):
        for j in range(EACH):
            rows = [
                got[pl.ds((k * FAR_Z + far) * EACH + j, FIRST, stride=LINES), :]
                for k in range(PER)
            ]
            rows = jnp.concatenate(rows, axis=0)
            high = rows.astype(jnp.bfloat16)
            rest = rows - high.astype(jnp.float32)
            middle = rest.astype(jnp.bfloat16)
            low = (rest - middle.astype(jnp.float32)).astype(jnp.bfloat16)
            terms = jnp.concatenate([low, middle, high], axis=0)
            sums = jnp.dot(picks, terms, preferred_element_type=jnp.float32)
            out[pl.ds(far * EACH + j, TILES, stride=FAR_Z * EACH), :] = sums


def gather(got):
    return pl.pallas_call(
        gather_kernel,
        out_shape=jax.ShapeDtypeStruct((TILES * FAR_Z * EACH, LANES), jnp.float32),
        compiler_params=pltpu.CompilerParams(vmem_limit_bytes=SMALL),
        name="gather",
    )(got)


def add_kernel(got, out):
    for far in range(FAR_Z):
        for near in range(NEAR_Y):
            for j in range(EACH):
                starts = [
                    ((y * NEAR_Y + near) * 8 * FAR_Z + far) * EACH + j for y in range(FAR_Y)
                ]
                rows = [got[pl.ds(start, 8, stride=FAR_Z * EACH), :] for start in starts]
                out[pl.ds(far * TILES + near * EACH + j, 8, stride=8), :] = sum(rows[1:], rows[0])


def finish_kernel(got, out):
    parts = [got[pl.ds(far * TILES, TILES), :] for far in range(FAR_Z)]
    out[...] = sum(parts[1:], parts[0])


def add(kernel, got, rows):
    return pl.pallas_call(
        kernel,
        out_shape=jax.ShapeDtypeStruct((rows, LANES), jnp.float32),
        compiler_params=pltpu.CompilerParams(vmem_limit_bytes=SMALL),
        name="add",
    )(got)


def exchange(rows, axes, devices):
    each = rows.shape[0] // devices
    sent = rows.reshape(devices, each, 1, LANES)
    return lax.all_to_all(sent, axes, 0, 0, tiled=True).reshape(rows.shape)


def shards(amps, ints, partners, irrep_sizes, tile_slot):
    sent = products(irrep_sizes, tile_slot, partners[0], amps[0], ints[0])
    got = exchange(sent, ("near_z", "x", "core", "near_y"), FIRST)
    sums = gather(got)
    got = exchange(sums, ("far_y", "near_y"), 8)
    sums = add(add_kernel, got, FAR_Z * TILES)
    got = exchange(sums, ("far_z", "x", "core"), FAR_Z * 8)
    return add(finish_kernel, got, TILES)[None]


def solution(mesh):
    fine = Mesh(mesh.devices.reshape(4, FAR_Y, NEAR_Y, 2, FAR_Z, NEAR_Z), VIR + OCC)
    in_specs = (P(VIR, None, None), P(VIR, OCC, None, None), P(VIR, None), P(), P())
    out_specs = P(VIR, OCC, None)
    return jax.shard_map(shards, mesh=fine, in_specs=in_specs, out_specs=out_specs, check_vma=False)
```

```python
import jax
import jax.numpy as jnp
from jax import lax
from jax.experimental import pallas as pl
from jax.experimental.pallas import tpu as pltpu
from jax.sharding import Mesh
from jax.sharding import PartitionSpec as P

TILES = 64
PLANES = 12
NEAR_Y = 2
NEAR_Z = 3
FAR_Y = 8 // NEAR_Y
FAR_Z = PLANES // NEAR_Z
PER = 3
PIECES = 8 * NEAR_Y
EACH = TILES // PIECES
FIRST = PIECES * NEAR_Z
LINES = PER * FAR_Z * EACH + 1
LANES = 128
DEPTHS = (512, 1024, 1024, 1024, 256, 256)
STARTS = tuple(sum(DEPTHS[:step]) for step in range(len(DEPTHS)))
HALF = 384
ROOM = 56 * 1024 * 1024
SMALL = 16 * 1024 * 1024
VIR = ("x", "far_y", "near_y", "core")
OCC = ("far_z", "near_z")


def codes_row(sizes, slots, partners):
    y = lax.axis_index("far_y") * NEAR_Y + lax.axis_index("near_y")
    slot = (lax.axis_index("x") * 8 + y) * 2 + lax.axis_index("core")
    plane = lax.axis_index("far_z") * NEAR_Z + lax.axis_index("near_z")
    own = lax.fori_loop(
        0, TILES, lambda t, own: own + jnp.where(slots[t] == slot, t, 0), jnp.int32(0)
    )
    live = jnp.where(own >= sizes[0], sizes[1], sizes[0])
    lanes = lax.broadcasted_iota(jnp.int32, (1, LANES), 1)
    y = lanes % FAR_Y * NEAR_Y + lanes // FAR_Y % NEAR_Y
    slot_of = (lanes // 8 % 4 * 8 + y) * 2 + lanes // 32
    slot_of = jnp.where(lanes < TILES, slot_of, -2)
    row = jnp.zeros((1, LANES), jnp.float32)
    for k in range(PER):
        index = plane * PER + k
        target = jnp.where(index < live, slots[partners[index]], -1)
        row = jnp.where(slot_of == target, jnp.float32(k + 1), row)
    return row


def products_kernel(tables, amps, ints, out, left, right, total, held, sems, table_sems):
    copies = []
    for step, (start, depth) in enumerate(zip(STARTS, DEPTHS)):
        part = pl.ds(start, depth)
        copies.append(
            (
                pltpu.make_async_copy(amps.at[:, part], left.at[:, part], sems.at[0, step]),
                pltpu.make_async_copy(ints.at[:, part], right.at[:, part], sems.at[1, step]),
            )
        )
    small = [
        pltpu.make_async_copy(tables[i], held[i], table_sems.at[i]) for i in range(len(tables))
    ]
    for copy in copies[0]:
        copy.start()
    for copy in small:
        copy.start()
    for pair in copies[1:]:
        for copy in pair:
            copy.start()
    for copy in small:
        copy.wait()
    row = codes_row(*held)
    out[pl.ds(LINES - 1, FIRST, stride=LINES), :] = jnp.broadcast_to(row, (FIRST, LANES))
    for step, pair in enumerate(copies):
        for copy in pair:
            copy.wait()
        part = pl.ds(STARTS[step], DEPTHS[step])
        weights = jnp.concatenate([right[k, part, :] for k in range(PER)], axis=1)
        for half in range(2):
            rows = pl.ds(half * HALF, HALF)
            now = jnp.dot(left[rows, part], weights, preferred_element_type=jnp.float32)
            for k in range(PER):
                term = now[:, k * LANES : (k + 1) * LANES]
                total[k, rows, :] = term if step == 0 else total[k, rows, :] + term
    for far in range(FAR_Z):
        for near in range(NEAR_Z):
            for k in range(PER):
                for j in range(EACH):
                    start = TILES * (far * NEAR_Z + near) + j
                    line = near * PIECES * LINES + (k * FAR_Z + far) * EACH + j
                    out[pl.ds(line, PIECES, stride=LINES), :] = total[
                        k, pl.ds(start, PIECES, stride=EACH), :
                    ]


def products(sizes, slots, partners, amps, ints):
    pairs, depth = amps.shape
    anywhere = pl.BlockSpec(memory_space=pl.ANY)
    tables = (sizes, slots, partners)
    return pl.pallas_call(
        products_kernel,
        in_specs=[(anywhere,) * 3, anywhere, anywhere],
        out_specs=pl.BlockSpec(memory_space=pltpu.VMEM),
        out_shape=jax.ShapeDtypeStruct((FIRST * LINES, LANES), jnp.float32),
        scratch_shapes=[
            pltpu.VMEM((pairs, depth), jnp.bfloat16),
            pltpu.VMEM((PER, depth, LANES), jnp.bfloat16),
            pltpu.VMEM((PER, pairs, LANES), jnp.float32),
            [pltpu.SMEM(table.shape, jnp.int32) for table in tables],
            pltpu.SemaphoreType.DMA((2, len(DEPTHS))),
            pltpu.SemaphoreType.DMA((len(tables),)),
        ],
        compiler_params=pltpu.CompilerParams(vmem_limit_bytes=ROOM),
        name="products",
    )(tables, amps, ints)


def gather_kernel(got, out):
    codes = jnp.transpose(got[pl.ds(LINES - 1, FIRST, stride=LINES), :])[:TILES]
    picks = [(codes == jnp.float32(k + 1)).astype(jnp.float32) for k in range(PER)]
    picks = jnp.concatenate(picks * 3, axis=1).astype(jnp.bfloat16)
    for far in range(FAR_Z):
        for j in range(EACH):
            rows = [
                got[pl.ds((k * FAR_Z + far) * EACH + j, FIRST, stride=LINES), :]
                for k in range(PER)
            ]
            rows = jnp.concatenate(rows, axis=0)
            high = rows.astype(jnp.bfloat16)
            rest = rows - high.astype(jnp.float32)
            middle = rest.astype(jnp.bfloat16)
            low = (rest - middle.astype(jnp.float32)).astype(jnp.bfloat16)
            terms = jnp.concatenate([low, middle, high], axis=0)
            sums = jnp.dot(picks, terms, preferred_element_type=jnp.float32)
            for core in range(2):
                start = (core * FAR_Z + far) * 32 * EACH + j
                out[pl.ds(start, 32, stride=EACH), :] = sums[core * 32 : core * 32 + 32]


def gather(got):
    return pl.pallas_call(
        gather_kernel,
        out_shape=jax.ShapeDtypeStruct((TILES * FAR_Z * EACH, LANES), jnp.float32),
        compiler_params=pltpu.CompilerParams(vmem_limit_bytes=SMALL),
        name="gather",
    )(got)


def finish_kernel(got, out):
    half = PIECES // 2
    for core in range(2):
        for j in range(EACH):
            rows = [
                got[pl.ds(((core * FAR_Z + z) * half * FAR_Y + y) * EACH + j, half, stride=FAR_Y * EACH), :]
                for z in range(FAR_Z)
                for y in range(FAR_Y)
            ]
            out[pl.ds(core * half * EACH + j, half, stride=EACH), :] = sum(rows[1:], rows[0])


def add(kernel, got, rows):
    return pl.pallas_call(
        kernel,
        out_shape=jax.ShapeDtypeStruct((rows, LANES), jnp.float32),
        compiler_params=pltpu.CompilerParams(vmem_limit_bytes=SMALL),
        name="add",
    )(got)


def exchange(rows, axes, devices):
    each = rows.shape[0] // devices
    sent = rows.reshape(devices, each, 1, LANES)
    return lax.all_to_all(sent, axes, 0, 0, tiled=True).reshape(rows.shape)


def shards(amps, ints, partners, irrep_sizes, tile_slot):
    sent = products(irrep_sizes, tile_slot, partners[0], amps[0], ints[0])
    got = exchange(sent, ("near_z", "core", "x", "near_y"), FIRST)
    sums = gather(got)
    got = exchange(sums, ("core", "far_z", "x", "near_y", "far_y"), TILES * FAR_Z)
    return add(finish_kernel, got, TILES)[None]


def solution(mesh):
    fine = Mesh(mesh.devices.reshape(4, FAR_Y, NEAR_Y, 2, FAR_Z, NEAR_Z), VIR + OCC)
    in_specs = (P(VIR, None, None), P(VIR, OCC, None, None), P(VIR, None), P(), P())
    out_specs = P(VIR, OCC, None)
    return jax.shard_map(shards, mesh=fine, in_specs=in_specs, out_specs=out_specs, check_vma=False)
```
